32 devices in a mesh: chan: 4 (over y, x), tile: 8 (over z, core).
Axes of the slice: x: 2, y: 2, z: 4, core: 2. Of those that a mesh axis runs over, the one named last changes fastest.
Arguments:
- voltages: bfloat16 [2, 32, 2048, 512], P(None, None, ('chan', 'tile')), may hold values from -6 to 6
- tile_pairs: int32 [528, 2], replicated, may hold values from 0 to 31, as said below
Outputs:
- visibilities: float32 [528, 32, 64, 128], P(None, ('chan', 'tile'))
The draws below stay inside these ranges and needn't reach their ends.
Inputs may be any that keep to these rules, and one draw needn't show every extreme that they name: `tile_pairs`: every pair of panels (p, q) with p <= q occurs in exactly one row; in every row the first entry is at most the second.
All inputs are finite; a program needn't handle non-finite values.
Results may differ from the reference program's by a relative error of at most 0.0003.
Values may be sent and summed in bfloat16 or wider, within the bound.
A program may use at most 320 MiB of HBM per device.

```python
import jax
import jax.numpy as jnp
import numpy as np
from jax import lax

INPUTS = 2048
PANELS = 32
SPECTRA = 512
CHANS = 32
PANEL = 64


def draw_tile_pairs(key, part):
    listed = np.array([[row, col] for row in range(PANELS) for col in range(row, PANELS)], dtype=np.int32)
    order = jax.random.permutation(jax.random.fold_in(key, 11), listed.shape[0])
    return jnp.asarray(listed)[order]


def level_of(key, extent, split, smallest, top_value):
    gain = 1.0
    for position, blocks in split:
        heights = jax.random.uniform(jax.random.fold_in(jax.random.fold_in(key, 6), position), (blocks,), jnp.float32, smallest / len(split), top_value / len(split))
        gain = gain * jnp.repeat(jnp.exp(heights), extent[position] // blocks).reshape((-1,) + (1,) * (len(extent) - 1 - position))
    return gain


def gaussian(stream_key, dims, width, most, cuts=(), kind=jnp.bfloat16):
    gain = level_of(stream_key, dims, cuts, -0.22, 0.18) if cuts else 1.0
    entries = jax.random.normal(stream_key, dims, jnp.float32) * width * gain
    return jnp.minimum(jnp.maximum(entries, -most), most).astype(kind)


def setup_inputs(seed: int = 0) -> dict:
    key_list = jax.random.split(jax.random.key(seed), 3)
    return {
        "voltages": gaussian(key_list[0], (2, CHANS, INPUTS, SPECTRA), 1.0, 6.0, ((2, 32),)),
        "tile_pairs": draw_tile_pairs(jax.random.fold_in(key_list[2], 71), 0),
    }


def reference(voltages, tile_pairs):
    arranged = voltages.reshape(2, CHANS, PANELS, PANEL, SPECTRA)

    def one_slot(pair):
        row_data = lax.dynamic_index_in_dim(arranged, pair[0].astype(jnp.int32), 2, keepdims=False).astype(jnp.float32)
        col_data = lax.dynamic_index_in_dim(arranged, pair[1].astype(jnp.int32), 2, keepdims=False).astype(jnp.float32)
        hp = lax.Precision.HIGHEST
        real_part = jnp.einsum("fmt,fnt->fmn", row_data[0], col_data[0], precision=hp) + jnp.einsum("fmt,fnt->fmn", row_data[1], col_data[1], precision=hp)
        imag_part = jnp.einsum("fmt,fnt->fmn", row_data[1], col_data[0], precision=hp) - jnp.einsum("fmt,fnt->fmn", row_data[0], col_data[1], precision=hp)
        return jnp.concatenate((real_part, imag_part), axis=-1)

    result = lax.map(one_slot, tile_pairs)
    return result * (SPECTRA ** -0.5)
```

```python
import functools

import jax
import jax.numpy as jnp
from jax import lax
from jax.experimental import pallas as pl
from jax.experimental.pallas import tpu as pltpu
from jax.sharding import PartitionSpec as P

PANELS = 32
PANEL = 64
GROUP = 4
GROUPS = PANELS // GROUP
MESH = pl.DeviceIdType.MESH


def flipped(index, mask):
    for bit in range(mask.bit_length()):
        if mask >> bit & 1:
            index = index + (1 << bit) * (1 - 2 * (index // (1 << bit) % 2))
    return index


def send_order(chan_size, tile_size):
    half = tile_size // 2
    order = []
    for chan_mask in range(chan_size):
        for tile_mask in range(half):
            order.append((chan_mask, tile_mask + half))
            if chan_mask or tile_mask:
                order.append((chan_mask, tile_mask))
    return order


def turn_kernel(sizes, pairs_ref, volt_ref, turned_ref, slots_ref, send_sem, recv_sem, own_sem):
    chan_size, tile_size = sizes
    chan, tile = lax.axis_index("chan"), lax.axis_index("tile")
    me = chan * tile_size + tile
    inputs = volt_ref.shape[2]
    here = turned_ref.shape[1]
    order = send_order(chan_size, tile_size)

    barrier = pltpu.get_barrier_semaphore()
    for masks in order:
        to = (flipped(chan, masks[0]), flipped(tile, masks[1]))
        pl.semaphore_signal(barrier, inc=1, device_id=to, device_id_type=MESH)
    pl.semaphore_wait(barrier, len(order))

    rows = pl.ds(pl.multiple_of(me * inputs, inputs), inputs)
    own = pltpu.make_async_copy(volt_ref.at[:, pl.ds(me * here, here)], turned_ref.at[:, :, rows], own_sem)
    copies = []
    for masks in order:
        to = (flipped(chan, masks[0]), flipped(tile, masks[1]))
        flat = to[0] * tile_size + to[1]
        copies.append(
            pltpu.make_async_remote_copy(
                src_ref=volt_ref.at[:, pl.ds(flat * here, here)],
                dst_ref=turned_ref.at[:, :, rows],
                send_sem=send_sem.at[len(copies)],
                recv_sem=recv_sem.at[len(copies)],
                device_id=to,
                device_id_type=MESH,
            )
        )
        copies[-1].start()
    own.start()

    code = pairs_ref[:, 0:1] * PANELS + pairs_ref[:, 1:2]
    slot = lax.broadcasted_iota(jnp.int32, (code.shape[0], 128), 0)
    for part in range(PANELS * PANELS // 128):
        wanted = lax.broadcasted_iota(jnp.int32, (code.shape[0], 128), 1) + part * 128
        slots_ref[:, part * 128 : part * 128 + 128] = jnp.sum(
            jnp.where(code == wanted, slot, 0), axis=0, keepdims=True
        )

    own.wait()
    for copy in copies:
        copy.wait()


def product_kernel(slots_ref, turned_ref, out_ref, left, right, stage, load_sem, out_sem):
    here, spectra = turned_ref.shape[1], turned_ref.shape[3]
    width = GROUP * PANEL
    scale = spectra ** (-0.5)
    for f in range(here):
        loads = []
        for g in range(GROUPS):
            rows = pl.ds(g * width, width)
            for part in range(2):
                loads.append(
                    pltpu.make_async_copy(
                        turned_ref.at[part, f, rows],
                        left.at[rows, pl.ds(part * spectra, spectra)],
                        load_sem.at[2 * g + part],
                    )
                )
                loads[-1].start()
        for h in range(GROUPS):
            loads[2 * h].wait()
            loads[2 * h + 1].wait()
            for q in range(GROUP):
                first = (h * GROUP + q) * PANEL
                real_part = left[first : first + PANEL, :spectra]
                imag_part = left[first : first + PANEL, spectra:]
                right[q * 2 * PANEL : q * 2 * PANEL + PANEL, :spectra] = real_part
                right[q * 2 * PANEL : q * 2 * PANEL + PANEL, spectra:] = imag_part
                right[q * 2 * PANEL + PANEL : (q + 1) * 2 * PANEL, :spectra] = -imag_part
                right[q * 2 * PANEL + PANEL : (q + 1) * 2 * PANEL, spectra:] = real_part

            def block(g, carry):
                at = h * (h + 1) // 2 + g
                product = (
                    lax.dot_general(
                        left[pl.ds(pl.multiple_of(g * width, width), width), :],
                        right[...],
                        (((1,), (1,)), ((), ())),
                        preferred_element_type=jnp.float32,
                    )
                    * scale
                )
                for m in range(GROUP):
                    for q in range(GROUP):
                        stage[at, m * GROUP + q] = product[
                            m * PANEL : (m + 1) * PANEL, q * 2 * PANEL : (q + 1) * 2 * PANEL
                        ]
                for m in range(GROUP):
                    for q in range(GROUP):

                        def put():
                            slot = slots_ref[0, (g * GROUP + m) * PANELS + h * GROUP + q]
                            pltpu.make_async_copy(stage.at[at, m * GROUP + q], out_ref.at[slot, f], out_sem).start()

                        if m <= q:
                            put()
                        else:
                            pl.when(g < h)(put)
                return carry

            lax.fori_loop(0, h + 1, block, 0)

        def drain(index, carry):
            pltpu.make_async_copy(stage.at[0], stage.at[0], out_sem).wait()
            return carry

        lax.fori_loop(0, PANELS * (PANELS + 1) // 2 // (GROUP * GROUP), drain, 0)


def body(sizes, voltages, tile_pairs):
    chan_size, tile_size = sizes
    parts, chans, inputs, spectra = voltages.shape
    here = chans // (chan_size * tile_size)
    all_inputs = PANELS * PANEL
    count = chan_size * tile_size - 1
    pairs = tile_pairs.shape[0]
    turned, slots = pl.pallas_call(
        functools.partial(turn_kernel, sizes),
        out_shape=(
            jax.ShapeDtypeStruct((parts, here, all_inputs, spectra), voltages.dtype),
            jax.ShapeDtypeStruct((1, PANELS * PANELS), jnp.int32),
        ),
        in_specs=[pl.BlockSpec(memory_space=pltpu.VMEM), pl.BlockSpec(memory_space=pl.ANY)],
        out_specs=(pl.BlockSpec(memory_space=pl.ANY), pl.BlockSpec(memory_space=pltpu.VMEM)),
        scratch_shapes=[
            pltpu.SemaphoreType.DMA((count,)),
            pltpu.SemaphoreType.DMA((count,)),
            pltpu.SemaphoreType.DMA,
        ],
        compiler_params=pltpu.CompilerParams(
            collective_id=0, has_side_effects=True, vmem_limit_bytes=32 * 1024 * 1024
        ),
        name="corner_turn",
    )(tile_pairs, voltages)
    width = GROUP * PANEL
    return pl.pallas_call(
        product_kernel,
        out_shape=jax.ShapeDtypeStruct((pairs, here, PANEL, 2 * PANEL), jnp.float32),
        in_specs=[pl.BlockSpec(memory_space=pltpu.SMEM), pl.BlockSpec(memory_space=pl.ANY)],
        out_specs=pl.BlockSpec(memory_space=pl.ANY),
        scratch_shapes=[
            pltpu.VMEM((all_inputs, parts * spectra), voltages.dtype),
            pltpu.VMEM((2 * width, parts * spectra), voltages.dtype),
            pltpu.VMEM((GROUPS * (GROUPS + 1) // 2, GROUP * GROUP, PANEL, 2 * PANEL), jnp.float32),
            pltpu.SemaphoreType.DMA((2 * GROUPS,)),
            pltpu.SemaphoreType.DMA,
        ],
        compiler_params=pltpu.CompilerParams(vmem_limit_bytes=48 * 1024 * 1024),
        name="tile_products",
    )(slots, turned)


def solution(mesh):
    sizes = (mesh.shape["chan"], mesh.shape["tile"])
    return jax.shard_map(
        functools.partial(body, sizes),
        mesh=mesh,
        in_specs=(P(None, None, ("chan", "tile"), None), P()),
        out_specs=P(None, ("chan", "tile"), None, None),
        check_vma=False,
    )
```

```python
import functools

import jax
import jax.numpy as jnp
from jax import lax
from jax.experimental import pallas as pl
from jax.experimental.pallas import tpu as pltpu
from jax.sharding import PartitionSpec as P

PANELS = 32
PANEL = 64
LATE = 1
MESH = pl.DeviceIdType.MESH
MIB = 1024 * 1024


def flipped(index, mask, size):
    bit, result = 1, 0
    while bit < size:
        result = result + (index // bit + mask // bit) % 2 * bit
        bit *= 2
    return result


def group_at(sizes, chan, tile, place):
    half = sizes[1] // 2
    return flipped(chan, place // 2, sizes[0]) * 2 + (tile // half + place) % 2


def pair_index(a, b):
    count = lambda groups: groups * (groups - 1) // 2
    return count(b) + a


def send_order(sizes):
    half = sizes[1] // 2
    order = []
    for chan_mask in range(sizes[0]):
        for tile_mask in range(half):
            order.append((chan_mask, tile_mask + half))
            if chan_mask or tile_mask:
                order.append((chan_mask, tile_mask))
    return order


def multiply(turned_ref, right_ref, store, g, h, width):
    spectra = turned_ref.shape[3]
    rows = pl.ds(pl.multiple_of(g * width, width), width)
    total = None
    for part in range(2):
        term = lax.dot_general(
            turned_ref[part, 0, rows, :],
            right_ref[h, part],
            (((1,), (1,)), ((), ())),
            preferred_element_type=jnp.float32,
        )
        total = term if total is None else total + term
    total = total * spectra ** (-0.5)
    per = width // PANEL
    for m in range(per):
        for q in range(per):
            store(m * per + q, total[m * PANEL : (m + 1) * PANEL, q * 2 * PANEL : (q + 1) * 2 * PANEL])


def turn_kernel(
    sizes, pairs_ref, volt_ref, turned_ref, right_ref, tiles_ref, slots_ref, send_sem, recv_sem, own_sem
):
    chan, tile = lax.axis_index("chan"), lax.axis_index("tile")
    me = chan * sizes[1] + tile
    inputs = volt_ref.shape[2]
    groups = 2 * sizes[0]
    width = turned_ref.shape[2] // groups
    per = width // PANEL
    order = send_order(sizes)

    barrier = pltpu.get_barrier_semaphore()
    for masks in order:
        to = (flipped(chan, masks[0], sizes[0]), flipped(tile, masks[1], sizes[1]))
        pl.semaphore_signal(barrier, inc=1, device_id=to, device_id_type=MESH)
    pl.semaphore_wait(barrier, len(order))

    rows = pl.ds(pl.multiple_of(me * inputs, inputs), inputs)
    copies = {}
    for number, masks in enumerate(order):
        to = (flipped(chan, masks[0], sizes[0]), flipped(tile, masks[1], sizes[1]))
        copies[masks] = pltpu.make_async_remote_copy(
            src_ref=volt_ref.at[:, pl.ds(to[0] * sizes[1] + to[1], 1)],
            dst_ref=turned_ref.at[:, :, rows],
            send_sem=send_sem.at[number],
            recv_sem=recv_sem.at[number],
            device_id=to,
            device_id_type=MESH,
        )
        copies[masks].start()
    own = pltpu.make_async_copy(volt_ref.at[:, pl.ds(me, 1)], turned_ref.at[:, :, rows], own_sem)
    own.start()

    listed = pairs_ref.shape[1]
    code = pairs_ref[0:1, :] * PANELS + pairs_ref[1:2, :]
    code = jnp.transpose(jnp.broadcast_to(code, (128, listed)))
    slot = lax.broadcasted_iota(jnp.int32, (listed, 128), 0)
    lane = lax.broadcasted_iota(jnp.int32, (listed, 128), 1)
    for part in range(PANELS * PANELS // 128):
        slots_ref[:, part * 128 : part * 128 + 128] = jnp.sum(
            jnp.where(code == lane + part * 128, slot, 0), axis=0, keepdims=True
        )

    own.wait()
    for place in range(groups):
        for masks in order:
            if masks[0] * 2 + masks[1] // (sizes[1] // 2) == place:
                copies[masks].wait_recv()
        x = group_at(sizes, chan, tile, place)
        for q in range(per):
            panel = pl.ds(pl.multiple_of(x * width + q * PANEL, PANEL), PANEL)
            real_part = turned_ref[0, 0, panel, :]
            imag_part = turned_ref[1, 0, panel, :]
            first, second = pl.ds(q * 2 * PANEL, PANEL), pl.ds(q * 2 * PANEL + PANEL, PANEL)
            right_ref[x, 0, first, :] = real_part
            right_ref[x, 0, second, :] = -imag_part
            right_ref[x, 1, first, :] = imag_part
            right_ref[x, 1, second, :] = real_part
        if place < groups - LATE:

            def block(other, carry):
                y = group_at(sizes, chan, tile, other)
                at = jnp.where(other == place, pair_index(0, groups - LATE) + place, pair_index(other, place))

                def store(number, value):
                    tiles_ref[at, number] = value

                multiply(turned_ref, right_ref, store, jnp.minimum(x, y), jnp.maximum(x, y), width)
                return carry

            lax.fori_loop(0, place + 1, block, 0)

    for masks in order:
        copies[masks].wait_send()


def place_kernel(sizes, slots_ref, turned_ref, right_ref, tiles_ref, out_ref, last_ref, sem):
    chan, tile = lax.axis_index("chan"), lax.axis_index("tile")
    groups = 2 * sizes[0]
    width = turned_ref.shape[2] // groups
    per = width // PANEL
    early = groups - LATE

    def put(source, x, y):
        g, h = (x, y) if x is y else (jnp.minimum(x, y), jnp.maximum(x, y))
        base = g * (per * PANELS) + h * per
        for m in range(per):
            for q in range(m if x is y else 0, per):
                slot = slots_ref[0, base + m * PANELS + q]
                pltpu.make_async_copy(source.at[m * per + q], out_ref.at[slot, 0], sem).start()

    ids = [group_at(sizes, chan, tile, place) for place in range(groups)]
    ready = [(a, b) for b in range(early) for a in range(b)]
    ready += [(a, a) for a in range(early)]
    late = [(a, b) for b in range(early, groups) for a in range(b + 1)]
    share = -(-len(ready) // len(late))
    for number, (a, b) in enumerate(late):
        for k in range(number * share, min((number + 1) * share, len(ready))):
            put(tiles_ref.at[k], ids[ready[k][0]], ids[ready[k][1]])

        def store(place, value):
            last_ref[number, place] = value

        multiply(
            turned_ref, right_ref, store, jnp.minimum(ids[a], ids[b]), jnp.maximum(ids[a], ids[b]), width
        )
        put(last_ref.at[number], ids[a], ids[b])

    def drain(index, carry):
        pltpu.make_async_copy(last_ref.at[0], last_ref.at[0], sem).wait()
        return carry

    lax.fori_loop(0, out_ref.shape[0] // (per * per), drain, 0)


def body(sizes, voltages, tile_pairs):
    parts, chans, inputs, spectra = voltages.shape
    devices = sizes[0] * sizes[1]
    groups = 2 * sizes[0]
    per = PANELS // groups
    listed = tile_pairs.shape[0]
    if chans != devices or listed % (per * per):
        raise ValueError("unsupported sizes")
    early = groups - LATE
    vmem = pl.BlockSpec(memory_space=pltpu.VMEM)
    results = pl.pallas_call(
        functools.partial(turn_kernel, sizes),
        out_shape=(
            pltpu.VMEM((parts, 1, PANELS * PANEL, spectra), voltages.dtype),
            pltpu.VMEM((groups, 2, 2 * per * PANEL, spectra), voltages.dtype),
            pltpu.VMEM((early * (early + 1) // 2, per * per, PANEL, 2 * PANEL), jnp.float32),
            pltpu.VMEM((1, PANELS * PANELS), jnp.int32),
        ),
        in_specs=[vmem, pl.BlockSpec(memory_space=pltpu.HBM)],
        out_specs=(vmem,) * 4,
        scratch_shapes=[
            pltpu.SemaphoreType.DMA((devices - 1,)),
            pltpu.SemaphoreType.DMA((devices - 1,)),
            pltpu.SemaphoreType.DMA,
        ],
        compiler_params=pltpu.CompilerParams(
            collective_id=0, has_side_effects=True, vmem_limit_bytes=12 * MIB
        ),
        name="corner_turn",
    )(tile_pairs.T, pltpu.with_memory_space_constraint(voltages, pltpu.HBM))
    turned, right, tiles, slots = results
    return pl.pallas_call(
        functools.partial(place_kernel, sizes),
        out_shape=jax.ShapeDtypeStruct((listed, 1, PANEL, 2 * PANEL), jnp.float32),
        in_specs=[pl.BlockSpec(memory_space=pltpu.SMEM), vmem, vmem, vmem],
        out_specs=pl.BlockSpec(memory_space=pl.ANY),
        scratch_shapes=[
            pltpu.VMEM((groups * LATE - LATE * (LATE - 1) // 2, per * per, PANEL, 2 * PANEL), jnp.float32),
            pltpu.SemaphoreType.DMA,
        ],
        compiler_params=pltpu.CompilerParams(vmem_limit_bytes=16 * MIB),
        name="tile_placement",
    )(slots, turned, right, tiles)


def solution(mesh):
    sizes = (mesh.shape["chan"], mesh.shape["tile"])
    return jax.shard_map(
        functools.partial(body, sizes),
        mesh=mesh,
        in_specs=(P(None, None, ("chan", "tile"), None), P()),
        out_specs=P(None, ("chan", "tile"), None, None),
        check_vma=False,
    )
```

```python
import functools

import jax
import jax.numpy as jnp
from jax import lax
from jax.experimental import pallas as pl
from jax.experimental.pallas import tpu as pltpu
from jax.sharding import PartitionSpec as P

PANELS = 32
PANEL = 64
LATE = 1
MESH = pl.DeviceIdType.MESH
MIB = 1024 * 1024


def flipped(index, mask, size):
    bit, result = 1, 0
    while bit < size:
        result = result + (index // bit + mask // bit) % 2 * bit
        bit *= 2
    return result


def group_at(sizes, chan, tile, place):
    half = sizes[1] // 2
    return flipped(chan, place // 2, sizes[0]) * 2 + (tile // half + place) % 2


def pair_index(a, b):
    count = lambda groups: groups * (groups - 1) // 2
    return count(b) + a


def send_order(sizes):
    half = sizes[1] // 2
    masks = [(chan_mask, tile_mask) for chan_mask in range(sizes[0]) for tile_mask in range(half)]
    near, far = masks[1:], [(chan_mask, tile_mask + half) for chan_mask, tile_mask in masks]
    order, nears = [], 0
    for fars in range(len(far)):
        order.append(far[fars])
        while nears < len(near) and 2 * nears < 3 * (fars + 1):
            order.append(near[nears])
            nears += 1
    return order


def multiply(turned_ref, right_ref, g, h, width):
    spectra = turned_ref.shape[3]
    rows = pl.ds(pl.multiple_of(g * width, width), width)
    total = None
    for part in range(2):
        term = lax.dot_general(
            turned_ref[part, 0, rows, :],
            right_ref[h, part],
            (((1,), (1,)), ((), ())),
            preferred_element_type=jnp.float32,
        )
        total = term if total is None else total + term
    total = total * spectra ** (-0.5)
    per = width // PANEL
    return jnp.stack(
        [
            total[m * PANEL : (m + 1) * PANEL, q * 2 * PANEL : (q + 1) * 2 * PANEL]
            for m in range(per)
            for q in range(per)
        ]
    )


def turn_kernel(
    sizes, pairs_hbm, volt_ref, turned_ref, right_ref, tiles_ref, slots_ref, pairs_ref, send_sem, recv_sem, own_sem
):
    chan, tile = lax.axis_index("chan"), lax.axis_index("tile")
    me = chan * sizes[1] + tile
    inputs = volt_ref.shape[2]
    groups = 2 * sizes[0]
    width = turned_ref.shape[2] // groups
    per = width // PANEL
    order = send_order(sizes)
    chans = [flipped(chan, mask, sizes[0]) for mask in range(sizes[0])]
    tiles = [flipped(tile, mask, sizes[1]) for mask in range(sizes[1])]

    barrier = pltpu.get_barrier_semaphore()
    for masks in order:
        to = (chans[masks[0]], tiles[masks[1]])
        pl.semaphore_signal(barrier, inc=1, device_id=to, device_id_type=MESH)
    fetch = pltpu.make_async_copy(pairs_hbm, pairs_ref, own_sem.at[1])
    fetch.start()
    pl.semaphore_wait(barrier, len(order))

    rows = pl.ds(pl.multiple_of(me * inputs, inputs), inputs)
    copies = {}
    for number, masks in enumerate(order):
        to = (chans[masks[0]], tiles[masks[1]])
        copies[masks] = pltpu.make_async_remote_copy(
            src_ref=volt_ref.at[:, pl.ds(to[0] * sizes[1] + to[1], 1)],
            dst_ref=turned_ref.at[:, :, rows],
            send_sem=send_sem.at[number],
            recv_sem=recv_sem.at[number],
            device_id=to,
            device_id_type=MESH,
        )
        copies[masks].start()
    own = pltpu.make_async_copy(volt_ref.at[:, pl.ds(me, 1)], turned_ref.at[:, :, rows], own_sem.at[0])
    own.start()

    fetch.wait()
    listed = pairs_ref.shape[1]
    code = pairs_ref[0:1, :] * PANELS + pairs_ref[1:2, :]
    code = jnp.transpose(jnp.broadcast_to(code, (128, listed)))
    slot = lax.broadcasted_iota(jnp.int32, (listed, 128), 0)
    lane = lax.broadcasted_iota(jnp.int32, (listed, 128), 1)
    for part in range(PANELS * PANELS // 128):
        slots_ref[:, part * 128 : part * 128 + 128] = jnp.sum(
            jnp.where(code == lane + part * 128, slot, 0), axis=0, keepdims=True
        )

    own.wait()
    for place in range(groups):
        for masks in order:
            if masks[0] * 2 + masks[1] // (sizes[1] // 2) == place:
                copies[masks].wait_recv()
        x = group_at(sizes, chan, tile, place)
        rows = pl.ds(pl.multiple_of(x * width, width), width)
        real_part, imag_part = turned_ref[0, 0, rows, :], turned_ref[1, 0, rows, :]
        cut = [slice(q * PANEL, (q + 1) * PANEL) for q in range(per)]
        right_ref[x, 0] = jnp.concatenate([piece for c in cut for piece in (real_part[c], -imag_part[c])], axis=0)
        right_ref[x, 1] = jnp.concatenate([piece for c in cut for piece in (imag_part[c], real_part[c])], axis=0)
        if place < groups - LATE:

            def block(other, carry):
                y = group_at(sizes, chan, tile, other)
                at = jnp.where(other == place, pair_index(0, groups - LATE) + place, pair_index(other, place))
                tiles_ref[at] = multiply(turned_ref, right_ref, jnp.minimum(x, y), jnp.maximum(x, y), width)
                return carry

            lax.fori_loop(0, place + 1, block, 0)

    for masks in order:
        copies[masks].wait_send()


def place_kernel(sizes, slots_vmem, turned_ref, right_ref, tiles_ref, out_ref, last_ref, slots_ref, slots_sem, sem):
    fetch = pltpu.make_async_copy(slots_vmem, slots_ref, slots_sem)
    fetch.start()
    chan, tile = lax.axis_index("chan"), lax.axis_index("tile")
    groups = 2 * sizes[0]
    width = turned_ref.shape[2] // groups
    per = width // PANEL
    early = groups - LATE

    def put(source, x, y):
        g, h = (x, y) if x is y else (jnp.minimum(x, y), jnp.maximum(x, y))
        base = g * (per * PANELS) + h * per
        for m in range(per):
            for q in range(m if x is y else 0, per):
                slot = slots_ref[0, base + m * PANELS + q]
                pltpu.make_async_copy(source.at[m * per + q], out_ref.at[slot, 0], sem).start()

    ids = [group_at(sizes, chan, tile, place) for place in range(groups)]
    ready = [(a, b) for b in range(early) for a in range(b)]
    ready += [(a, a) for a in range(early)]
    late = [(a, b) for b in range(early, groups) for a in range(b + 1)]
    share = -(-len(ready) // len(late))
    for number, (a, b) in enumerate(late):
        last_ref[number] = multiply(
            turned_ref, right_ref, jnp.minimum(ids[a], ids[b]), jnp.maximum(ids[a], ids[b]), width
        )
        if number == 0:
            fetch.wait()
        for k in range(number * share, min((number + 1) * share, len(ready))):
            put(tiles_ref.at[k], ids[ready[k][0]], ids[ready[k][1]])
        put(last_ref.at[number], ids[a], ids[b])

    def drain(index, carry):
        pltpu.make_async_copy(last_ref.at[0], last_ref.at[0], sem).wait()
        return carry

    lax.fori_loop(0, out_ref.shape[0] // (per * per), drain, 0)


def body(sizes, voltages, tile_pairs):
    parts, chans, inputs, spectra = voltages.shape
    devices = sizes[0] * sizes[1]
    groups = 2 * sizes[0]
    per = PANELS // groups
    listed = tile_pairs.shape[0]
    if chans != devices or listed % (per * per):
        raise ValueError("unsupported sizes")
    early = groups - LATE
    vmem = pl.BlockSpec(memory_space=pltpu.VMEM)
    results = pl.pallas_call(
        functools.partial(turn_kernel, sizes),
        out_shape=(
            pltpu.VMEM((parts, 1, PANELS * PANEL, spectra), voltages.dtype),
            pltpu.VMEM((groups, 2, 2 * per * PANEL, spectra), voltages.dtype),
            pltpu.VMEM((early * (early + 1) // 2, per * per, PANEL, 2 * PANEL), jnp.float32),
            pltpu.VMEM((1, PANELS * PANELS), jnp.int32),
        ),
        in_specs=[pl.BlockSpec(memory_space=pltpu.HBM)] * 2,
        out_specs=(vmem,) * 4,
        scratch_shapes=[
            pltpu.VMEM((2, listed), jnp.int32),
            pltpu.SemaphoreType.DMA((devices - 1,)),
            pltpu.SemaphoreType.DMA((devices - 1,)),
            pltpu.SemaphoreType.DMA((2,)),
        ],
        compiler_params=pltpu.CompilerParams(
            collective_id=0, has_side_effects=True, vmem_limit_bytes=12 * MIB
        ),
        name="corner_turn",
    )(
        pltpu.with_memory_space_constraint(tile_pairs.T, pltpu.HBM),
        pltpu.with_memory_space_constraint(voltages, pltpu.HBM),
    )
    turned, right, tiles, slots = results
    return pl.pallas_call(
        functools.partial(place_kernel, sizes),
        out_shape=jax.ShapeDtypeStruct((listed, 1, PANEL, 2 * PANEL), jnp.float32),
        in_specs=[vmem] * 4,
        out_specs=pl.BlockSpec(memory_space=pl.ANY),
        scratch_shapes=[
            pltpu.VMEM((groups * LATE - LATE * (LATE - 1) // 2, per * per, PANEL, 2 * PANEL), jnp.float32),
            pltpu.SMEM((1, PANELS * PANELS), jnp.int32),
            pltpu.SemaphoreType.DMA,
            pltpu.SemaphoreType.DMA,
        ],
        compiler_params=pltpu.CompilerParams(vmem_limit_bytes=16 * MIB),
        name="tile_placement",
    )(slots, turned, right, tiles)


def solution(mesh):
    sizes = (mesh.shape["chan"], mesh.shape["tile"])
    return jax.shard_map(
        functools.partial(body, sizes),
        mesh=mesh,
        in_specs=(P(None, None, ("chan", "tile"), None), P()),
        out_specs=P(None, ("chan", "tile"), None, None),
        check_vma=False,
    )
```

```python
import functools

import jax
import jax.numpy as jnp
from jax import lax
from jax.experimental import pallas as pl
from jax.experimental.pallas import tpu as pltpu
from jax.sharding import PartitionSpec as P

PANELS = 32
PANEL = 64
LATE = 1
MESH = pl.DeviceIdType.MESH
MIB = 1024 * 1024


def flipped(index, mask, size):
    bit, result = 1, 0
    while bit < size:
        result = result + (index // bit + mask // bit) % 2 * bit
        bit *= 2
    return result


def group_at(sizes, chan, tile, place):
    half = sizes[1] // 2
    return flipped(chan, place // 2, sizes[0]) * 2 + (tile // half + place) % 2


def pair_index(a, b):
    count = lambda groups: groups * (groups - 1) // 2
    return count(b) + a


def send_order(sizes, lead):
    half = sizes[1] // 2
    masks = [(chan_mask, tile_mask) for chan_mask in range(sizes[0]) for tile_mask in range(half)]
    near, far = masks[1:], [(chan_mask, tile_mask + half) for chan_mask, tile_mask in masks]
    order = []
    for number, masks in enumerate(far):
        order.append(masks)
        order += near[number * lead : (number + 1) * lead]
    return order


def multiply(turned_ref, right_ref, g, h, width):
    spectra = turned_ref.shape[3]
    rows = pl.ds(pl.multiple_of(g * width, width), width)
    total = None
    for part in range(2):
        term = lax.dot_general(
            turned_ref[part, 0, rows, :],
            right_ref[h, part],
            (((1,), (1,)), ((), ())),
            preferred_element_type=jnp.float32,
        )
        total = term if total is None else total + term
    total = total * spectra ** (-0.5)
    per = width // PANEL
    return jnp.stack(
        [
            total[m * PANEL : (m + 1) * PANEL, q * 2 * PANEL : (q + 1) * 2 * PANEL]
            for m in range(per)
            for q in range(per)
        ]
    )


def turn_kernel(
    sizes, pairs_hbm, volt_ref, turned_ref, right_ref, tiles_ref, slots_ref, pairs_ref, send_sem, recv_sem, own_sem
):
    chan, tile = lax.axis_index("chan"), lax.axis_index("tile")
    me = chan * sizes[1] + tile
    inputs = volt_ref.shape[2]
    groups = 2 * sizes[0]
    width = turned_ref.shape[2] // groups
    per = width // PANEL
    order = send_order(sizes, 1)
    chans = [flipped(chan, mask, sizes[0]) for mask in range(sizes[0])]
    tiles = [flipped(tile, mask, sizes[1]) for mask in range(sizes[1])]

    barrier = pltpu.get_barrier_semaphore()
    for masks in order:
        to = (chans[masks[0]], tiles[masks[1]])
        pl.semaphore_signal(barrier, inc=1, device_id=to, device_id_type=MESH)
    fetch = pltpu.make_async_copy(pairs_hbm, pairs_ref, own_sem.at[1])
    fetch.start()
    pl.semaphore_wait(barrier, len(order))

    rows = pl.ds(pl.multiple_of(me * inputs, inputs), inputs)
    copies = {}
    for number, masks in enumerate(order):
        to = (chans[masks[0]], tiles[masks[1]])
        copies[masks] = pltpu.make_async_remote_copy(
            src_ref=volt_ref.at[:, pl.ds(to[0] * sizes[1] + to[1], 1)],
            dst_ref=turned_ref.at[:, :, rows],
            send_sem=send_sem.at[number],
            recv_sem=recv_sem.at[number],
            device_id=to,
            device_id_type=MESH,
        )

    middle = (tile // (sizes[1] // 2) + tile // (sizes[1] // 4)) % 2

    @pl.when(middle == 1)
    def _():
        for masks in order:
            copies[masks].start()

    @pl.when(middle == 0)
    def _():
        for masks in send_order(sizes, 2):
            copies[masks].start()

    own = pltpu.make_async_copy(volt_ref.at[:, pl.ds(me, 1)], turned_ref.at[:, :, rows], own_sem.at[0])
    own.start()

    fetch.wait()
    listed = pairs_ref.shape[1]
    code = pairs_ref[0:1, :] * PANELS + pairs_ref[1:2, :]
    code = jnp.transpose(jnp.broadcast_to(code, (128, listed)))
    slot = lax.broadcasted_iota(jnp.int32, (listed, 128), 0)
    lane = lax.broadcasted_iota(jnp.int32, (listed, 128), 1)
    for part in range(PANELS * PANELS // 128):
        slots_ref[:, part * 128 : part * 128 + 128] = jnp.sum(
            jnp.where(code == lane + part * 128, slot, 0), axis=0, keepdims=True
        )

    own.wait()
    for place in range(groups):
        for masks in order:
            if masks[0] * 2 + masks[1] // (sizes[1] // 2) == place:
                copies[masks].wait_recv()
        x = group_at(sizes, chan, tile, place)
        rows = pl.ds(pl.multiple_of(x * width, width), width)
        real_part, imag_part = turned_ref[0, 0, rows, :], turned_ref[1, 0, rows, :]
        cut = [slice(q * PANEL, (q + 1) * PANEL) for q in range(per)]
        right_ref[x, 0] = jnp.concatenate([piece for c in cut for piece in (real_part[c], -imag_part[c])], axis=0)
        right_ref[x, 1] = jnp.concatenate([piece for c in cut for piece in (imag_part[c], real_part[c])], axis=0)
        if place < groups - LATE:

            def block(other, carry):
                y = group_at(sizes, chan, tile, other)
                at = jnp.where(other == place, pair_index(0, groups - LATE) + place, pair_index(other, place))
                tiles_ref[at] = multiply(turned_ref, right_ref, jnp.minimum(x, y), jnp.maximum(x, y), width)
                return carry

            lax.fori_loop(0, place + 1, block, 0)

    for masks in order:
        copies[masks].wait_send()


def place_kernel(sizes, slots_vmem, turned_ref, right_ref, tiles_ref, out_ref, last_ref, slots_ref, slots_sem, sem):
    fetch = pltpu.make_async_copy(slots_vmem, slots_ref, slots_sem)
    fetch.start()
    chan, tile = lax.axis_index("chan"), lax.axis_index("tile")
    groups = 2 * sizes[0]
    width = turned_ref.shape[2] // groups
    per = width // PANEL
    early = groups - LATE

    def put(source, x, y):
        g, h = (x, y) if x is y else (jnp.minimum(x, y), jnp.maximum(x, y))
        base = g * (per * PANELS) + h * per
        for m in range(per):
            for q in range(m if x is y else 0, per):
                slot = slots_ref[0, base + m * PANELS + q]
                pltpu.make_async_copy(source.at[m * per + q], out_ref.at[slot, 0], sem).start()

    ids = [group_at(sizes, chan, tile, place) for place in range(groups)]
    ready = [(a, b) for b in range(early) for a in range(b)]
    ready += [(a, a) for a in range(early)]
    late = [(a, b) for b in range(early, groups) for a in range(b + 1)]
    share = -(-len(ready) // len(late))
    for number, (a, b) in enumerate(late):
        last_ref[number] = multiply(
            turned_ref, right_ref, jnp.minimum(ids[a], ids[b]), jnp.maximum(ids[a], ids[b]), width
        )
        if number == 0:
            fetch.wait()
        for k in range(number * share, min((number + 1) * share, len(ready))):
            put(tiles_ref.at[k], ids[ready[k][0]], ids[ready[k][1]])
        put(last_ref.at[number], ids[a], ids[b])

    def drain(index, carry):
        pltpu.make_async_copy(last_ref.at[0], last_ref.at[0], sem).wait()
        return carry

    lax.fori_loop(0, out_ref.shape[0] // (per * per), drain, 0)


def body(sizes, voltages, tile_pairs):
    parts, chans, inputs, spectra = voltages.shape
    devices = sizes[0] * sizes[1]
    groups = 2 * sizes[0]
    per = PANELS // groups
    listed = tile_pairs.shape[0]
    if chans != devices or listed % (per * per):
        raise ValueError("unsupported sizes")
    early = groups - LATE
    vmem = pl.BlockSpec(memory_space=pltpu.VMEM)
    results = pl.pallas_call(
        functools.partial(turn_kernel, sizes),
        out_shape=(
            pltpu.VMEM((parts, 1, PANELS * PANEL, spectra), voltages.dtype),
            pltpu.VMEM((groups, 2, 2 * per * PANEL, spectra), voltages.dtype),
            pltpu.VMEM((early * (early + 1) // 2, per * per, PANEL, 2 * PANEL), jnp.float32),
            pltpu.VMEM((1, PANELS * PANELS), jnp.int32),
        ),
        in_specs=[pl.BlockSpec(memory_space=pltpu.HBM)] * 2,
        out_specs=(vmem,) * 4,
        scratch_shapes=[
            pltpu.VMEM((2, listed), jnp.int32),
            pltpu.SemaphoreType.DMA((devices - 1,)),
            pltpu.SemaphoreType.DMA((devices - 1,)),
            pltpu.SemaphoreType.DMA((2,)),
        ],
        compiler_params=pltpu.CompilerParams(
            collective_id=0, has_side_effects=True, vmem_limit_bytes=12 * MIB
        ),
        name="corner_turn",
    )(
        pltpu.with_memory_space_constraint(tile_pairs.T, pltpu.HBM),
        pltpu.with_memory_space_constraint(voltages, pltpu.HBM),
    )
    turned, right, tiles, slots = results
    return pl.pallas_call(
        functools.partial(place_kernel, sizes),
        out_shape=jax.ShapeDtypeStruct((listed, 1, PANEL, 2 * PANEL), jnp.float32),
        in_specs=[vmem] * 4,
        out_specs=pl.BlockSpec(memory_space=pl.ANY),
        scratch_shapes=[
            pltpu.VMEM((groups * LATE - LATE * (LATE - 1) // 2, per * per, PANEL, 2 * PANEL), jnp.float32),
            pltpu.SMEM((1, PANELS * PANELS), jnp.int32),
            pltpu.SemaphoreType.DMA,
            pltpu.SemaphoreType.DMA,
        ],
        compiler_params=pltpu.CompilerParams(vmem_limit_bytes=16 * MIB),
        name="tile_placement",
    )(slots, turned, right, tiles)


def solution(mesh):
    sizes = (mesh.shape["chan"], mesh.shape["tile"])
    return jax.shard_map(
        functools.partial(body, sizes),
        mesh=mesh,
        in_specs=(P(None, None, ("chan", "tile"), None), P()),
        out_specs=P(None, ("chan", "tile"), None, None),
        check_vma=False,
    )
```
